128 devices in a mesh: gx: 8 (over z, x_hi), gz: 16 (over y, x_lo, core).
Axes of the slice: x: 4 (x_hi: 2, x_lo: 2; x = x_hi * 2 + x_lo), y: 4, z: 4, core: 2. Of those that a mesh axis runs over, the one named last changes fastest.
Arguments:
- field: float32 [3, 256, 256, 512], P(None, ('gx', 'gz')), may hold values from -4 to 4
- atom_vel: float32 [3, 2, 256, 65536], P(None, None, 'gx', 'gz'), may hold values from -6 to 6
- cell_ids: int32 [2, 256, 65536], P(None, 'gx', 'gz'), may hold values from 0 to 31, as said below
- fluid: int32 [2, 256, 65536], P(None, 'gx', 'gz'), may hold values from 0 to 1, as said below
Outputs:
- new_field: float32 [3, 256, 256, 512], P(None, ('gx', 'gz'))
- new_atoms: float32 [3, 2, 256, 65536], P(None, None, 'gx', 'gz')
The draws below stay inside these ranges and needn't reach their ends.
Inputs may be any that keep to these rules, and one draw needn't show every extreme that they name: `cell_ids`: an atom's cell lies in its own brick's spanwise range. Some intersection cells are wall region, and all atoms in them have fluid 0.
All inputs are finite; a program needn't handle non-finite values.
Results may differ from the reference program's by a relative error of at most 0.000076.
Values sent between devices are 32-bit elements; how exact they have to be, the bound alone decides.
No kernel may reach another device: no remote copies, remote signals or barrier semaphores. Data moves between devices by JAX's collectives and lax.ppermute only.
A program may use at most 192 MiB of HBM per device.

```python
import jax
import jax.numpy as jnp

CZ = 32
NY = 256
OY = 2
ATOM_ROW = 4096
STEPS = 2
NX = 256
NZ = 512
ATOM_Z = 65536


def atom_layout(key):
    ids = jax.random.randint(jax.random.fold_in(key, 11), (OY, NX, ATOM_Z), 0, CZ)
    walled = jax.random.randint(jax.random.fold_in(key, 12), (OY, NX, NZ), 0, 8) == 0
    base = jax.random.randint(jax.random.fold_in(key, 13), (OY, NX, ATOM_Z), 0, 4) > 0
    spans = (jnp.arange(ATOM_Z, dtype=jnp.int32) // ATOM_ROW)[None, None, :] * CZ + ids
    inside_wall = jnp.take_along_axis(walled, spans, axis=2)
    fluid_mask = jnp.where(inside_wall, 0, base.astype(jnp.int32)).astype(jnp.int32)
    return (ids.astype(jnp.int32), fluid_mask)


def draw_cell_ids(key, part):
    return atom_layout(key)[0]


def draw_fluid(key, part):
    return atom_layout(key)[1]


def level_of(own_key, dims, cuts, smallest, high):
    loudness, own = 1.0, jax.random.fold_in(own_key, 6)
    for position, shards_of in cuts:
        steps = jnp.exp(jax.random.uniform(jax.random.fold_in(own, position), (shards_of,), jnp.float32, smallest / len(cuts), high / len(cuts)))
        loudness = loudness * jnp.repeat(steps, dims[position] // shards_of).reshape([-1 if axis == position else 1 for axis in range(len(dims))])
    return loudness


def normal_values(stream_key, shape, scale, limit, pieces=(), kind=jnp.bfloat16):
    drawn = jax.random.normal(stream_key, shape, jnp.float32) * scale
    if len(pieces) > 0:
        drawn = level_of(stream_key, shape, pieces, -0.22, 0.18) * drawn
    return jnp.clip(drawn, min=-limit, max=limit).astype(kind)


def setup_inputs(seed: int = 0) -> dict:
    streams_of = jax.random.split(jax.random.key(seed), 5)
    field = normal_values(streams_of[0], (3, NX, NY, NZ), 0.5, 4.0, ((1, 128),), jnp.float32)
    atom_vel = normal_values(streams_of[1], (3, OY, NX, ATOM_Z), 1.0, 6.0, ((2, 8), (3, 16)), jnp.float32)
    cell_ids = draw_cell_ids(jax.random.fold_in(streams_of[4], 71), 0)
    fluid = draw_fluid(jax.random.fold_in(streams_of[4], 71), 0)
    return {"field": field, "atom_vel": atom_vel, "cell_ids": cell_ids, "fluid": fluid}


VISCOUS = 0.15
COURANT = 0.05
PLATE_SPEED = 1.0


def update(velocity, x_ahead, x_behind, z_ahead, z_behind):
    below_row = jnp.concatenate([jnp.zeros_like(velocity[:, :, :1]), velocity[:, :, :-1]], 2)
    top_wall = jnp.concatenate([jnp.full_like(velocity[:1, :, :1], PLATE_SPEED), jnp.zeros_like(velocity[1:, :, :1])], 0)
    above_row = jnp.concatenate([velocity[:, :, 1:], top_wall], 2)
    laplace = x_ahead + x_behind + z_ahead + z_behind + below_row + above_row - 6.0 * velocity
    transport = velocity[0:1] * (x_ahead - x_behind) + velocity[1:2] * (above_row - below_row) + velocity[2:3] * (z_ahead - z_behind)
    return velocity + VISCOUS * laplace - COURANT * transport


def reference(field, atom_vel, cell_ids, fluid):
    weight = fluid.astype(jnp.float32)
    rows = jnp.arange(OY, dtype=jnp.int32)[:, None, None]
    streams = jnp.arange(NX, dtype=jnp.int32)[None, :, None]
    blocks = (jnp.arange(ATOM_Z, dtype=jnp.int32) // ATOM_ROW)[None, None, :]
    spans = blocks * CZ + cell_ids
    segment = ((streams * OY + rows) * NZ + spans).reshape(-1)
    total = NX * OY * NZ
    weighted = (atom_vel * weight[None]).reshape(3, -1).T
    sums = jax.ops.segment_sum(weighted, segment, total).T.reshape(3, NX, OY, NZ)
    counts = jax.ops.segment_sum(weight.reshape(-1), segment, total).reshape(1, NX, OY, NZ)
    mean = sums / jnp.maximum(counts, 1.0)
    seeded = jnp.where(counts > 0, mean, field[:, :, :OY])
    velocity = jnp.concatenate([seeded, field[:, :, OY:]], 2)
    for step in range(STEPS):
        velocity = update(velocity, jnp.roll(velocity, -1, 1), jnp.roll(velocity, 1, 1), jnp.roll(velocity, -1, 3), jnp.roll(velocity, 1, 3))
    delta = (velocity[:, :, :OY] - mean).reshape(3, -1)
    correction = delta[:, segment].reshape(3, OY, NX, ATOM_Z)
    return velocity, atom_vel + weight[None] * correction
```

```python
import functools

import jax
import jax.numpy as jnp
from jax import lax
from jax.experimental import pallas as pl
from jax.experimental.pallas import tpu as pltpu
from jax.sharding import PartitionSpec as P

CZ = 32
OY = 2
LANES = 128
TILE = 8
GROUP = 16
LOW = 16
FIRST = 64
SECOND = 104

VISCOUS = 0.15
COURANT = 0.05
PLATE_SPEED = 1.0

ROW_AXES = ("gx", "gz")


def means_kernel(vel_ref, ids_ref, fluid_ref, out_ref, key_ref, one_ref, *, atoms):
    columns = atoms // LANES
    lane = lax.broadcasted_iota(jnp.int32, (TILE, LANES), 1)

    def window(j):
        return pl.ds(pl.multiple_of(j * LANES, LANES), LANES)

    def prepare(j, carry):
        at = window(j)
        cell = jnp.where(fluid_ref[0, :, at] > 0, ids_ref[0, :, at], -1)
        key_ref[:, at] = cell
        one_ref[:, at] = lax.shift_left(jnp.int32(1), (cell & 3) * 8)
        return carry

    lax.fori_loop(0, columns, prepare, 0, unroll=8)
    out = jnp.zeros((TILE, LANES), jnp.float32)
    for first in range(0, CZ, GROUP):

        def body(j, totals):
            at = window(j)
            cell, one = key_ref[:, at], one_ref[:, at]
            v = [vel_ref[c, 0, :, at] for c in range(3)]
            totals = list(totals)
            for k in range(GROUP):
                hit = cell == first + k
                for c in range(3):
                    totals[3 * k + c] = totals[3 * k + c] + jnp.where(hit, v[c], 0.0)
            quad = lax.shift_right_arithmetic(cell, 2)
            for q in range(GROUP // 4):
                totals[3 * GROUP + q] = totals[3 * GROUP + q] + jnp.where(
                    quad == first // 4 + q, one, 0
                )
            return tuple(totals)

        zero = [jnp.zeros((TILE, LANES), jnp.float32)] * (3 * GROUP)
        zero += [jnp.zeros((TILE, LANES), jnp.int32)] * (GROUP // 4)
        totals = lax.fori_loop(0, columns, body, tuple(zero), unroll=4)
        for k in range(GROUP):
            packed = totals[3 * GROUP + k // 4]
            count = lax.shift_right_logical(packed, (k % 4) * 8) & 255
            count = jnp.sum(count.astype(jnp.float32), axis=1, keepdims=True)
            divisor = jnp.maximum(count, 1.0)
            for c in range(3):
                total = jnp.sum(totals[3 * k + c], axis=1, keepdims=True)
                out = jnp.where(lane == c * CZ + first + k, total / divisor, out)
            out = jnp.where(lane == 3 * CZ + first + k, count, out)
    out_ref[...] = out


def cell_means(vel, ids, fluid):
    _, _, nx, atoms = vel.shape
    assert atoms // LANES < 256
    atom_block = pl.BlockSpec((1, TILE, atoms), lambda r, x: (r, x, 0))
    return pl.pallas_call(
        functools.partial(means_kernel, atoms=atoms),
        grid=(OY, nx // TILE),
        in_specs=[
            pl.BlockSpec((3, 1, TILE, atoms), lambda r, x: (0, r, x, 0)),
            atom_block,
            atom_block,
        ],
        out_specs=pl.BlockSpec((TILE, LANES), lambda r, x: (x, r)),
        out_shape=jax.ShapeDtypeStruct((nx, OY * LANES), jnp.float32),
        scratch_shapes=[pltpu.VMEM((TILE, atoms), jnp.int32)] * 2,
        cost_estimate=pl.CostEstimate(flops=10**8, bytes_accessed=30 * 10**6, transcendentals=0),
        name="cell_means",
    )(vel, ids, fluid)


def constrain_kernel(vel_ref, ids_ref, fluid_ref, new_ref, mean_ref, out_ref, *, atoms):
    delta = new_ref[...] - mean_ref[...]
    for j in range(atoms // LANES):
        at = pl.ds(j * LANES, LANES)
        cell = ids_ref[0, :, at]
        weight = fluid_ref[0, :, at].astype(jnp.float32)
        for c in range(3):
            step = jnp.take_along_axis(delta, cell + c * CZ, axis=1)
            out_ref[c, 0, :, at] = vel_ref[c, 0, :, at] + weight * step


def constrain(vel, ids, fluid, new, mean):
    _, _, nx, atoms = vel.shape
    vel_block = pl.BlockSpec((3, 1, TILE, atoms), lambda r, x: (0, r, x, 0))
    atom_block = pl.BlockSpec((1, TILE, atoms), lambda r, x: (r, x, 0))
    cell_block = pl.BlockSpec((TILE, LANES), lambda r, x: (x, r))
    return pl.pallas_call(
        functools.partial(constrain_kernel, atoms=atoms),
        grid=(OY, nx // TILE),
        in_specs=[vel_block, atom_block, atom_block, cell_block, cell_block],
        out_specs=vel_block,
        out_shape=jax.ShapeDtypeStruct(vel.shape, vel.dtype),
        cost_estimate=pl.CostEstimate(flops=10**7, bytes_accessed=15 * 10**6, transcendentals=0),
        name="constrain",
    )(vel, ids, fluid, new, mean)


def plane_update(read, below, above, plane):
    centre = [read(c, plane) for c in range(3)]
    speed = [COURANT * u for u in centre]
    ahead = [VISCOUS - s for s in speed]
    behind = [VISCOUS + s for s in speed]
    nz = centre[0].shape[-1]
    fresh = []
    for c in range(3):
        u = centre[c]
        along_x = read(c, plane + 1) * ahead[0] + read(c, plane - 1) * behind[0]
        along_y = above(c, plane, u) * ahead[1] + below(c, plane, u) * behind[1]
        along_z = pltpu.roll(u, nz - 1, 1) * ahead[2] + pltpu.roll(u, 1, 1) * behind[2]
        fresh.append((1.0 - 6.0 * VISCOUS) * u + along_x + (along_y + along_z))
    return fresh


def two_steps_kernel(*refs, copies, segments, lo, hi, ny, n_in, low_rows):
    ins, out_ref = refs[:n_in], refs[n_in]
    start_ref, step_ref, new_ref, in_sem, out_sem = refs[n_in + 1 :]
    tiles = (hi - lo) // TILE
    nz = start_ref.shape[-1]

    pending = {}
    for number, (segment, source, plane, at, to, count) in enumerate(copies):
        copy = pltpu.make_async_copy(
            ins[source].at[:, :, pl.ds(at, count), :],
            start_ref.at[:, pl.ds(plane, 2), pl.ds(to, count), :],
            in_sem.at[number],
        )
        copy.start()
        pending.setdefault(segment, []).append(copy)
    outgoing = []
    if low_rows is not None:
        outgoing.append(
            pltpu.make_async_copy(
                ins[low_rows], out_ref.at[:, :, pl.ds(0, TILE), :], out_sem.at[0]
            )
        )
        outgoing[0].start()

    if lo == 0:
        for ref, planes in ((start_ref, 6), (step_ref, 4)):
            ref[:, :, pl.ds(TILE, TILE), :] = jnp.zeros((3, planes, TILE, nz), jnp.float32)
    if hi == ny:
        for ref, planes in ((start_ref, 6), (step_ref, 4)):
            at = pl.ds((tiles + 2) * TILE, TILE)
            ref[0, :, at, :] = jnp.full((planes, TILE, nz), PLATE_SPEED, jnp.float32)
            ref[1:, :, at, :] = jnp.zeros((2, planes, TILE, nz), jnp.float32)

    row = lax.broadcasted_iota(jnp.int32, (TILE, nz), 0)

    def readers(ref, t):
        def tile(c, plane, step):
            at = pl.ds(pl.multiple_of((t + step) * TILE, TILE), TILE)
            return ref[c, plane, at, :]

        def read(c, plane):
            return tile(c, plane, 0)

        def below(c, plane, u):
            return pltpu.roll(jnp.where(row == TILE - 1, tile(c, plane, -1), u), 1, 0)

        def above(c, plane, u):
            return pltpu.roll(jnp.where(row == 0, tile(c, plane, 1), u), TILE - 1, 0)

        return read, below, above

    def first_step(t):
        read, below, above = readers(start_ref, t)
        for plane in range(4):
            fresh = plane_update(read, below, above, plane + 1)
            for c in range(3):
                step_ref[c, plane, pl.ds(pl.multiple_of(t * TILE, TILE), TILE), :] = fresh[c]

    def second_step(t):
        read, below, above = readers(step_ref, t)
        for plane in range(2):
            fresh = plane_update(read, below, above, plane + 1)
            for c in range(3):
                at = pl.ds(pl.multiple_of((t - 2) * TILE, TILE), TILE)
                new_ref[c, plane, at, :] = fresh[c]

    def both_steps(t, carry):
        first_step(t)
        second_step(t - 1)
        return carry

    done_first, done_second = (1 if lo == 0 else 0), 1
    for segment, last_tile in enumerate(segments):
        for copy in pending.get(segment, []):
            copy.wait()
        end_first = tiles + 1 if hi == ny else tiles + 2
        reach_first = min(last_tile - 1, end_first) if segment < len(segments) - 1 else end_first
        reach_second = min(reach_first - 1, tiles + 1)
        while done_first < reach_first and done_second >= done_first:
            done_first += 1
            first_step(done_first)
        head = done_second
        if done_first == done_second + 1:
            begin = done_first + 1
        else:
            while done_first < min(reach_first, done_second + 1):
                done_first += 1
                first_step(done_first)
            begin = done_first + 1
        if reach_first >= begin:
            lax.fori_loop(begin, reach_first + 1, both_steps, 0)
            done_first = reach_first
            done_second = max(done_second, reach_first - 1)
        if segment == len(segments) - 1:
            while done_second < tiles + 1:
                done_second += 1
                second_step(done_second)
        if done_second > head:
            at, count = (head - 1) * TILE, (done_second - head) * TILE
            copy = pltpu.make_async_copy(
                new_ref.at[:, :, pl.ds(at, count), :],
                out_ref.at[:, :, pl.ds(at + (lo if out_ref.shape[2] == ny else 0), count), :],
                out_sem.at[len(outgoing)],
            )
            copy.start()
            outgoing.append(copy)
    for copy in outgoing:
        copy.wait()


def two_steps(own, before, after, lo, hi, ny, cuts=(), into=None, low=None, whole=True):
    nz = own[0][0].shape[-1]
    ins, copies = [], []
    floor, ceiling = max(lo - TILE, 0), min(hi + TILE, ny)
    edges = [floor] + [cut for cut in cuts if floor < cut < ceiling] + [ceiling]
    for plane, pieces in ((0, before), (2, own), (4, after)):
        for array, first in pieces:
            last = first + array.shape[2]
            used = False
            for segment, (a, b) in enumerate(zip(edges[:-1], edges[1:])):
                a, b = max(a, first), min(b, last)
                if a < b:
                    copies.append(
                        (segment, len(ins), plane, a - first, a - lo + 2 * TILE, b - a)
                    )
                    used = True
            if used:
                ins.append(array)
    segments = [(edge - lo) // TILE + 1 for edge in edges[1:]]
    low_rows = None
    if low is not None:
        low_rows = len(ins)
        ins.append(low)
    aliases = {}
    if into is not None:
        aliases = {len(ins): 0}
        ins.append(into)
    copies.sort(key=lambda copy: copy[0])
    span = hi - lo
    anywhere = pl.BlockSpec(memory_space=pl.ANY)
    return pl.pallas_call(
        functools.partial(
            two_steps_kernel,
            copies=copies,
            segments=segments,
            lo=lo,
            hi=hi,
            ny=ny,
            n_in=len(ins),
            low_rows=low_rows,
        ),
        in_specs=[anywhere] * len(ins),
        out_specs=anywhere,
        out_shape=jax.ShapeDtypeStruct((3, 2, ny if whole else span, nz), jnp.float32),
        scratch_shapes=[
            pltpu.VMEM((3, 6, span + 4 * TILE, nz), jnp.float32),
            pltpu.VMEM((3, 4, span + 4 * TILE, nz), jnp.float32),
            pltpu.VMEM((3, 2, span, nz), jnp.float32),
            pltpu.SemaphoreType.DMA((len(copies),)),
            pltpu.SemaphoreType.DMA((len(segments) + 1,)),
        ],
        input_output_aliases=aliases,
        compiler_params=pltpu.CompilerParams(vmem_limit_bytes=40 * 2**20),
        cost_estimate=pl.CostEstimate(
            flops=span * 10**6, bytes_accessed=span * 60 * 10**3, transcendentals=0
        ),
        name="two_steps",
    )(*ins)


def tie(value, *others):
    return lax.optimization_barrier((value,) + others)[0]


def local(field, atom_vel, cell_ids, fluid):
    _, planes, ny, nz = field.shape
    nx = atom_vel.shape[2]
    blocks = nz // CZ
    count = lax.axis_size("gx") * lax.axis_size("gz")
    forward = [(i, (i + 1) % count) for i in range(count)]
    backward = [(target, source) for source, target in forward]

    def halo(block):
        return lax.ppermute(block, ROW_AXES, forward), lax.ppermute(block, ROW_AXES, backward)

    first = halo(field[:, :, LOW:FIRST])
    means = cell_means(atom_vel, cell_ids, fluid)
    slab = lax.all_to_all(means, "gz", split_axis=0, concat_axis=0, tiled=True)
    second = halo(tie(field[:, :, FIRST:SECOND], slab))
    slab = slab.reshape(blocks, planes, OY, 4, CZ).transpose(3, 1, 2, 0, 4)
    slab = slab.reshape(4, planes, OY, nz)
    seeded = jnp.where(slab[3:] > 0, slab[:3], field[:, :, :OY])
    base = jnp.concatenate([seeded, field[:, :, OY:LOW]], 2)
    bottom = halo(base)
    own = [(base, 0), (field[:, :, LOW:], LOW)]
    low = two_steps(
        [(base, 0)], [(bottom[0], 0)], [(bottom[1], 0)], 0, TILE, ny, whole=False
    )
    back = low[:, :, :OY].reshape(3, planes, OY, blocks, CZ).transpose(3, 1, 2, 0, 4)
    back = jnp.pad(back, ((0, 0),) * 3 + ((0, 1), (0, 0))).reshape(blocks * planes, OY * LANES)
    back = lax.all_to_all(back, "gz", split_axis=0, concat_axis=0, tiled=True)
    third = halo(tie(field[:, :, SECOND:], back))
    new_atoms = constrain(atom_vel, cell_ids, fluid, back, means)

    before = [(bottom[0], 0), (first[0], LOW), (second[0], FIRST), (third[0], SECOND)]
    after = [(bottom[1], 0), (first[1], LOW), (second[1], FIRST), (third[1], SECOND)]
    part = two_steps([(field, 0)], before[:3], after[:3], TILE, SECOND - TILE, ny, (40, 72))
    new_field = two_steps(
        [(field, 0)],
        before[1:],
        after[1:],
        SECOND - TILE,
        ny,
        ny,
        (136, 176, 216),
        into=part,
        low=low,
    )
    return new_field, new_atoms


def solution(mesh):
    placed = (
        P(None, ("gx", "gz"), None, None),
        P(None, None, "gx", "gz"),
        P(None, "gx", "gz"),
        P(None, "gx", "gz"),
    )
    return jax.shard_map(
        local,
        mesh=mesh,
        in_specs=placed,
        out_specs=(P(None, ("gx", "gz"), None, None), P(None, None, "gx", "gz")),
        check_vma=False,
    )
```

```python
import functools

import jax
import jax.numpy as jnp
from jax import lax
from jax.experimental import pallas as pl
from jax.experimental.pallas import tpu as pltpu
from jax.sharding import PartitionSpec as P

CZ = 32
OY = 2
LANES = 128
TILE = 8
GROUP = 16
VMEM_BYTES = 64 * 2**20
LOW = 8
FIRST = 112
SECOND = 168
THIRD = 232

VISCOUS = 0.15
COURANT = 0.05
PLATE_SPEED = 1.0

ROW_AXES = ("gx", "gz")


def means_kernel(vel_ref, ids_ref, fluid_ref, field_ref, out_ref, send_ref, *refs, atoms, cuts):
    pieces, (key_ref, one_ref, held_ref, sem) = refs[:-4], refs[-4:]
    fetch = pltpu.make_async_copy(
        field_ref.at[:, :, pl.ds(cuts[0], cuts[-1] - cuts[0]), :], held_ref, sem.at[len(pieces)]
    )
    copies = [
        pltpu.make_async_copy(
            held_ref.at[:, :, pl.ds(a - cuts[0], b - a), :], piece, sem.at[number]
        )
        for number, (a, b, piece) in enumerate(zip(cuts[:-1], cuts[1:], pieces))
    ]

    @pl.when(pl.program_id(0) == 0)
    def _():
        fetch.start()

    @pl.when(pl.program_id(0) == 1)
    def _():
        fetch.wait()
        for copy in copies:
            copy.start()

    columns = atoms // LANES
    lane = lax.broadcasted_iota(jnp.int32, (TILE, LANES), 1)

    def window(j):
        return pl.ds(pl.multiple_of(j * LANES, LANES), LANES)

    for r in range(OY):

        def prepare(j, carry):
            at = window(j)
            cell = jnp.where(fluid_ref[r, :, at] > 0, ids_ref[r, :, at], -1)
            key_ref[:, at] = cell
            one_ref[:, at] = lax.shift_left(jnp.int32(1), (cell & 3) * 8)
            return carry

        lax.fori_loop(0, columns, prepare, 0, unroll=8)
        out = jnp.zeros((TILE, LANES), jnp.float32)
        for first in range(0, CZ, GROUP):

            def body(j, totals):
                at = window(j)
                cell, one = key_ref[:, at], one_ref[:, at]
                v = [vel_ref[c, r, :, at] for c in range(3)]
                totals = list(totals)
                for k in range(GROUP):
                    hit = cell == first + k
                    for c in range(3):
                        totals[3 * k + c] = totals[3 * k + c] + jnp.where(hit, v[c], 0.0)
                quad = lax.shift_right_arithmetic(cell, 2)
                for q in range(GROUP // 4):
                    totals[3 * GROUP + q] = totals[3 * GROUP + q] + jnp.where(
                        quad == first // 4 + q, one, 0
                    )
                return tuple(totals)

            zero = [jnp.zeros((TILE, LANES), jnp.float32)] * (3 * GROUP)
            zero += [jnp.zeros((TILE, LANES), jnp.int32)] * (GROUP // 4)
            totals = lax.fori_loop(0, columns, body, tuple(zero), unroll=4)
            for k in range(GROUP):
                packed = totals[3 * GROUP + k // 4]
                count = lax.shift_right_logical(packed, (k % 4) * 8) & 255
                count = jnp.sum(count.astype(jnp.float32), axis=1, keepdims=True)
                divisor = jnp.maximum(count, 1.0)
                for c in range(3):
                    total = jnp.sum(totals[3 * k + c], axis=1, keepdims=True)
                    out = jnp.where(lane == c * CZ + first + k, total / divisor, out)
                out = jnp.where(lane == 3 * CZ + first + k, count, out)
        out_ref[:, pl.ds(r * LANES, LANES)] = out
        for x in range(TILE):
            send_ref[x // 2, pl.ds((x % 2) * OY + r, 1), :] = out[x : x + 1]
            send_ref[x // 2, pl.ds(4 + (x % 2) * OY + r, 1), :] = out[x : x + 1]

    @pl.when(pl.program_id(0) == pl.num_programs(0) - 1)
    def _():
        for copy in copies:
            copy.wait()


def cell_means(vel, ids, fluid, field, cuts):
    _, _, nx, atoms = vel.shape
    assert atoms // LANES < 256 and nx >= 2 * TILE
    atom_block = pl.BlockSpec((OY, TILE, atoms), lambda x: (0, x, 0))
    return pl.pallas_call(
        functools.partial(means_kernel, atoms=atoms, cuts=cuts),
        grid=(nx // TILE,),
        in_specs=[
            pl.BlockSpec((3, OY, TILE, atoms), lambda x: (0, 0, x, 0)),
            atom_block,
            atom_block,
            pl.BlockSpec(memory_space=pltpu.HBM),
        ],
        out_specs=[
            pl.BlockSpec((TILE, OY * LANES), lambda x: (x, 0)),
            pl.BlockSpec((TILE // 2, 8, LANES), lambda x: (x, 0, 0)),
        ]
        + [pl.BlockSpec(memory_space=pltpu.HBM)] * (len(cuts) - 1),
        out_shape=[
            jax.ShapeDtypeStruct((nx, OY * LANES), jnp.float32),
            jax.ShapeDtypeStruct((nx // 2, 8, LANES), jnp.float32),
        ]
        + [
            jax.ShapeDtypeStruct((3, 2, b - a, field.shape[3]), jnp.float32)
            for a, b in zip(cuts[:-1], cuts[1:])
        ],
        scratch_shapes=[pltpu.VMEM((TILE, atoms), jnp.int32)] * 2
        + [
            pltpu.VMEM((3, 2, cuts[-1] - cuts[0], field.shape[3]), jnp.float32),
            pltpu.SemaphoreType.DMA((len(cuts),)),
        ],
        compiler_params=pltpu.CompilerParams(vmem_limit_bytes=VMEM_BYTES),
        cost_estimate=pl.CostEstimate(flops=10**8, bytes_accessed=40 * 10**6, transcendentals=0),
        name="cell_means",
    )(vel, ids, fluid, field)


def spread(block, k):
    return pltpu.roll(block, k % 4 * CZ, 1) if k % 4 else block


def seed_kernel(slab_ref, field_ref, out_ref):
    lane = lax.broadcasted_iota(jnp.int32, (TILE, LANES), 1) // CZ
    source = lax.broadcasted_iota(jnp.int32, (TILE, LANES), 0) // 2
    for q in range(slab_ref.shape[0] // 4):
        at = pl.ds(q * LANES, LANES)
        for r in range(OY):
            rows = [slab_ref[4 * q + m, pl.ds(p * OY + r, 1), :] for m in range(4) for p in range(2)]
            block = jnp.concatenate(rows, 0)
            turned = [spread(block, k) for k in range(4)]
            whole = []
            for c in range(4):
                part = jnp.zeros((TILE, LANES), jnp.float32)
                for m in range(4):
                    mine = jnp.logical_and(source == m, lane == m)
                    part = jnp.where(mine, turned[(m - c) % 4], part)
                part = part + pltpu.roll(part, 4, 0)
                whole.append(part + pltpu.roll(part, 2, 0))
            for c in range(3):
                for p in range(2):
                    kept = field_ref[c, p, pl.ds(r, 1), at]
                    fresh = jnp.where(whole[3][p : p + 1] > 0, whole[c][p : p + 1], kept)
                    out_ref[c, p, pl.ds(r, 1), at] = fresh
    out_ref[:, :, pl.ds(OY, LOW - OY), :] = field_ref[:, :, pl.ds(OY, LOW - OY), :]


def seed(slab, field):
    block = pl.BlockSpec((3, 2, LOW, field.shape[3]), lambda i: (0, 0, 0, 0))
    return pl.pallas_call(
        seed_kernel,
        grid=(1,),
        in_specs=[pl.BlockSpec(slab.shape, lambda i: (0, 0, 0)), block],
        out_specs=block,
        out_shape=jax.ShapeDtypeStruct((3, 2, LOW, field.shape[3]), jnp.float32),
        compiler_params=pltpu.CompilerParams(vmem_limit_bytes=VMEM_BYTES),
        name="seed",
    )(slab, field)


def write_back(low_ref, out_ref):
    lane = lax.broadcasted_iota(jnp.int32, (TILE, LANES), 1) // CZ
    row = lax.broadcasted_iota(jnp.int32, (TILE, LANES), 0)
    for q in range(out_ref.shape[0] // 4):
        at = pl.ds(q * LANES, LANES)
        for r in range(OY):
            block = jnp.zeros((TILE, LANES), jnp.float32)
            for c in range(3):
                even, odd = (low_ref[c, p, pl.ds(r, 1), at] for p in range(2))
                both = jnp.where(row % 2 == 0, even, odd)
                for m in range(4):
                    mine = jnp.logical_and(row // 2 == m, lane == c)
                    block = jnp.where(mine, spread(both, c - m), block)
            for m in range(4):
                for p in range(2):
                    line = block[2 * m + p : 2 * m + p + 1]
                    out_ref[4 * q + m, pl.ds(p * OY + r, 1), :] = line
                    out_ref[4 * q + m, pl.ds(4 + p * OY + r, 1), :] = line


def constrain_kernel(vel_ref, ids_ref, fluid_ref, new_ref, mean_ref, out_ref, *, atoms):
    for r in range(OY):
        rows = [new_ref[x // 2, pl.ds((x % 2) * OY + r, 1), :] for x in range(TILE)]
        delta = jnp.concatenate(rows, 0) - mean_ref[:, pl.ds(r * LANES, LANES)]
        for j in range(atoms // LANES):
            at = pl.ds(j * LANES, LANES)
            cell = ids_ref[r, :, at]
            weight = fluid_ref[r, :, at].astype(jnp.float32)
            for c in range(3):
                step = jnp.take_along_axis(delta, cell + c * CZ, axis=1)
                out_ref[c, r, :, at] = vel_ref[c, r, :, at] + weight * step


def constrain(vel, ids, fluid, new, mean):
    _, _, nx, atoms = vel.shape
    vel_block = pl.BlockSpec((3, OY, TILE, atoms), lambda x: (0, 0, x, 0))
    atom_block = pl.BlockSpec((OY, TILE, atoms), lambda x: (0, x, 0))
    return pl.pallas_call(
        functools.partial(constrain_kernel, atoms=atoms),
        grid=(nx // TILE,),
        in_specs=[
            vel_block,
            atom_block,
            atom_block,
            pl.BlockSpec((TILE // 2, 8, LANES), lambda x: (x, 0, 0)),
            pl.BlockSpec((TILE, OY * LANES), lambda x: (x, 0)),
        ],
        out_specs=vel_block,
        out_shape=jax.ShapeDtypeStruct(vel.shape, vel.dtype),
        compiler_params=pltpu.CompilerParams(vmem_limit_bytes=VMEM_BYTES),
        cost_estimate=pl.CostEstimate(flops=10**7, bytes_accessed=20 * 10**6, transcendentals=0),
        name="constrain",
    )(vel, ids, fluid, new, mean)


def plane_update(read, below, above, plane):
    centre = [read(c, plane) for c in range(3)]
    speed = [COURANT * u for u in centre]
    ahead = [VISCOUS - s for s in speed]
    behind = [VISCOUS + s for s in speed]
    nz = centre[0].shape[-1]
    fresh = []
    for c in range(3):
        u = centre[c]
        along_x = read(c, plane + 1) * ahead[0] + read(c, plane - 1) * behind[0]
        along_y = above(c, plane, u) * ahead[1] + below(c, plane, u) * behind[1]
        along_z = pltpu.roll(u, nz - 1, 1) * ahead[2] + pltpu.roll(u, 1, 1) * behind[2]
        fresh.append((1.0 - 6.0 * VISCOUS) * u + along_x + (along_y + along_z))
    return fresh


def two_steps_kernel(*refs, copies, segments, lo, hi, ny, n_in, low_rows):
    core_ref, ins, out_ref = refs[0], refs[1 : n_in + 1], refs[n_in + 1]
    start_ref, step_ref, new_ref, in_sem, out_sem = refs[-5:]
    tiles = (hi - lo) // TILE
    nz = start_ref.shape[-1]
    place = {"own": 2, "chip": 4 - 4 * core_ref[0], "far": 4 * core_ref[0]}

    pending = {}
    for number, (segment, source, plane, at, to, count) in enumerate(copies):
        copy = pltpu.make_async_copy(
            ins[source].at[:, :, pl.ds(at, count), :],
            start_ref.at[:, pl.ds(place[plane], 2), pl.ds(to, count), :],
            in_sem.at[number],
        )
        copy.start()
        pending.setdefault(segment, []).append(copy)
    outgoing = []
    if low_rows is not None:
        outgoing.append(
            pltpu.make_async_copy(
                ins[low_rows], out_ref.at[:, :, pl.ds(0, TILE), :], out_sem.at[0]
            )
        )
        outgoing[0].start()

    if lo == 0:
        for ref, planes in ((start_ref, 6), (step_ref, 4)):
            ref[:, :, pl.ds(TILE, TILE), :] = jnp.zeros((3, planes, TILE, nz), jnp.float32)
    if hi == ny:
        for ref, planes in ((start_ref, 6), (step_ref, 4)):
            at = pl.ds((tiles + 2) * TILE, TILE)
            ref[0, :, at, :] = jnp.full((planes, TILE, nz), PLATE_SPEED, jnp.float32)
            ref[1:, :, at, :] = jnp.zeros((2, planes, TILE, nz), jnp.float32)

    row = lax.broadcasted_iota(jnp.int32, (TILE, nz), 0)

    def readers(ref, t):
        def tile(c, plane, step):
            at = pl.ds(pl.multiple_of((t + step) * TILE, TILE), TILE)
            return ref[c, plane, at, :]

        def read(c, plane):
            return tile(c, plane, 0)

        def below(c, plane, u):
            return pltpu.roll(jnp.where(row == TILE - 1, tile(c, plane, -1), u), 1, 0)

        def above(c, plane, u):
            return pltpu.roll(jnp.where(row == 0, tile(c, plane, 1), u), TILE - 1, 0)

        return read, below, above

    def first_step(t):
        read, below, above = readers(start_ref, t)
        for plane in range(4):
            fresh = plane_update(read, below, above, plane + 1)
            for c in range(3):
                step_ref[c, plane, pl.ds(pl.multiple_of(t * TILE, TILE), TILE), :] = fresh[c]

    def second_step(t):
        read, below, above = readers(step_ref, t)
        for plane in range(2):
            fresh = plane_update(read, below, above, plane + 1)
            for c in range(3):
                at = pl.ds(pl.multiple_of((t - 2) * TILE, TILE), TILE)
                new_ref[c, plane, at, :] = fresh[c]

    def both_steps(t, carry):
        first_step(t)
        second_step(t - 1)
        return carry

    done_first, done_second = (1 if lo == 0 else 0), 1
    for segment, last_tile in enumerate(segments):
        for copy in pending.get(segment, []):
            copy.wait()
        end_first = tiles + 1 if hi == ny else tiles + 2
        reach_first = min(last_tile - 1, end_first) if segment < len(segments) - 1 else end_first
        reach_second = min(reach_first - 1, tiles + 1)
        while done_first < reach_first and done_second >= done_first:
            done_first += 1
            first_step(done_first)
        head = done_second
        if done_first == done_second + 1:
            begin = done_first + 1
        else:
            while done_first < min(reach_first, done_second + 1):
                done_first += 1
                first_step(done_first)
            begin = done_first + 1
        if reach_first >= begin:
            lax.fori_loop(begin, reach_first + 1, both_steps, 0)
            done_first = reach_first
            done_second = max(done_second, reach_first - 1)
        if segment == len(segments) - 1:
            while done_second < tiles + 1:
                done_second += 1
                second_step(done_second)
        if done_second > head:
            at, count = (head - 1) * TILE, (done_second - head) * TILE
            copy = pltpu.make_async_copy(
                new_ref.at[:, :, pl.ds(at, count), :],
                out_ref.at[:, :, pl.ds(at + (lo if out_ref.shape[2] == ny else 0), count), :],
                out_sem.at[len(outgoing)],
            )
            copy.start()
            outgoing.append(copy)
    if lo == 0:
        write_back(new_ref, refs[n_in + 2])
    for copy in outgoing:
        copy.wait()


def two_steps(core, own, chip, far, lo, hi, ny, cuts=(), into=None, low=None, whole=True):
    nz = own[0][0].shape[-1]
    ins, copies = [], []
    floor, ceiling = max(lo - TILE, 0), min(hi + TILE, ny)
    edges = [floor] + [cut for cut in cuts if floor < cut < ceiling] + [ceiling]
    for plane, pieces in (("own", own), ("chip", chip), ("far", far)):
        for array, first, *least in pieces:
            last = first + array.shape[2]
            used = False
            for segment, (a, b) in enumerate(zip(edges[:-1], edges[1:])):
                a, b = max(a, first, *least), min(b, last)
                if a < b:
                    copies.append(
                        (segment, len(ins), plane, a - first, a - lo + 2 * TILE, b - a)
                    )
                    used = True
            if used:
                ins.append(array)
    segments = [(edge - lo) // TILE + 1 for edge in edges[1:]]
    low_rows = None
    if low is not None:
        low_rows = len(ins)
        ins.append(low)
    aliases = {}
    if into is not None:
        aliases = {len(ins) + 1: 0}
        ins.append(into)
    copies.sort(key=lambda copy: copy[0])
    span = hi - lo
    anywhere = pl.BlockSpec(memory_space=pltpu.HBM)
    return pl.pallas_call(
        functools.partial(
            two_steps_kernel,
            copies=copies,
            segments=segments,
            lo=lo,
            hi=hi,
            ny=ny,
            n_in=len(ins),
            low_rows=low_rows,
        ),
        in_specs=[pl.BlockSpec(memory_space=pltpu.SMEM)] + [anywhere] * len(ins),
        out_specs=[anywhere] + [pl.BlockSpec(memory_space=pltpu.VMEM)] * (lo == 0),
        out_shape=[
            jax.ShapeDtypeStruct((3, 2, ny if whole else span, nz), jnp.float32),
            jax.ShapeDtypeStruct((nz // CZ, 8, LANES), jnp.float32),
        ][: 1 + (lo == 0)],
        scratch_shapes=[
            pltpu.VMEM((3, 6, span + 4 * TILE, nz), jnp.float32),
            pltpu.VMEM((3, 4, span + 4 * TILE, nz), jnp.float32),
            pltpu.VMEM((3, 2, span, nz), jnp.float32),
            pltpu.SemaphoreType.DMA((len(copies),)),
            pltpu.SemaphoreType.DMA((len(segments) + 1,)),
        ],
        input_output_aliases=aliases,
        compiler_params=pltpu.CompilerParams(vmem_limit_bytes=VMEM_BYTES),
        cost_estimate=pl.CostEstimate(
            flops=span * 10**6, bytes_accessed=span * 60 * 10**3, transcendentals=0
        ),
        name="two_steps",
    )(core, *ins)


def tie(value, *others):
    return lax.optimization_barrier((value,) + others)[0]


def local(field, atom_vel, cell_ids, fluid):
    ny = field.shape[2]
    count = lax.axis_size("gx") * lax.axis_size("gz")
    core = (lax.axis_index("gz") % 2).reshape(1)
    chip_pairs, far_pairs = [], []
    for i in range(0, count, 2):
        chip_pairs += [(i, i + 1), (i + 1, i)]
        far_pairs += [(i + 1, (i + 2) % count), ((i + 2) % count, i + 1)]

    def over_chip(block):
        return lax.ppermute(block, ROW_AXES, chip_pairs)

    def over_links(block):
        return lax.ppermute(block, ROW_AXES, far_pairs)

    def exchange(block):
        return lax.all_to_all(block, "gz", split_axis=0, concat_axis=0, tiled=True)

    first = over_links(field[:, :, LOW:FIRST])
    chip = over_chip(field)
    means, outgoing, *blocks = cell_means(
        atom_vel, cell_ids, fluid, field, (FIRST, SECOND, THIRD, ny)
    )
    slab = exchange(outgoing)
    base = seed(slab, field)
    base_chip, base_far = over_chip(base), over_links(base)
    second = over_links(tie(blocks[0], base_chip, base_far, first, chip))
    low, returned = two_steps(
        core,
        [(base, 0), (field, 0, LOW)],
        [(base_chip, 0), (chip, 0, LOW)],
        [(base_far, 0), (first, LOW)],
        0,
        TILE,
        ny,
        whole=False,
    )
    back = exchange(returned)
    own, beside = [(field, 0)], [(chip, 0)]
    far = [(base_far, 0), (first, LOW), (second, FIRST)]
    start, reach = TILE, FIRST - TILE
    (part,) = two_steps(core, own, beside, far[:2], start, reach, ny, (40, 72))
    third = over_links(tie(blocks[1], second, back, part))
    far.append((third, SECOND))
    new_atoms = constrain(atom_vel, cell_ids, fluid, back, means)
    start, reach = reach, SECOND - TILE
    (part,) = two_steps(core, own, beside, far[1:3], start, reach, ny, (136,), into=part)
    far.append((over_links(tie(blocks[2], part, new_atoms)), THIRD))
    start, reach = reach, THIRD - TILE
    (part,) = two_steps(core, own, beside, far[2:4], start, reach, ny, (192,), into=part)
    (new_field,) = two_steps(
        core, own, beside, far[3:], reach, ny, ny, into=part, low=low
    )
    return new_field, new_atoms


def solution(mesh):
    placed = (
        P(None, ("gx", "gz"), None, None),
        P(None, None, "gx", "gz"),
        P(None, "gx", "gz"),
        P(None, "gx", "gz"),
    )
    return jax.shard_map(
        local,
        mesh=mesh,
        in_specs=placed,
        out_specs=(P(None, ("gx", "gz"), None, None), P(None, None, "gx", "gz")),
        check_vma=False,
    )
```

```python
import functools

import jax
import jax.numpy as jnp
from jax import lax
from jax.experimental import pallas as pl
from jax.experimental.pallas import tpu as pltpu
from jax.sharding import PartitionSpec as P

CZ = 32
OY = 2
LANES = 128
TILE = 8
CHUNK = 2048
VMEM_BYTES = 64 * 2**20
LOW = 8
FIRST = 104
SECOND = 184

VISCOUS = 0.15
COURANT = 0.05
PLATE_SPEED = 1.0

ROW_AXES = ("gx", "gz")


def product(a, b, contract):
    return lax.dot_general(
        a, b, (((1,), (contract,)), ((), ())), preferred_element_type=jnp.float32
    )


def in_bfloat16(values):
    terms = []
    for _ in range(3):
        terms.append(values.astype(jnp.bfloat16).astype(jnp.float32))
        values = values - terms[-1]
    return terms


def means_kernel(vel_ref, ids_ref, fluid_ref, field_ref, out_ref, send_ref, *refs, atoms, cuts):
    pieces, (held_ref, sem) = refs[:-2], refs[-2:]
    fetch = pltpu.make_async_copy(
        field_ref.at[:, :, pl.ds(cuts[0], cuts[-1] - cuts[0]), :], held_ref, sem.at[len(pieces)]
    )
    copies = [
        pltpu.make_async_copy(
            held_ref.at[:, :, pl.ds(a - cuts[0], b - a), :], piece, sem.at[number]
        )
        for number, (a, b, piece) in enumerate(zip(cuts[:-1], cuts[1:], pieces))
    ]

    @pl.when(pl.program_id(0) == 0)
    def _():
        fetch.start()

    @pl.when(pl.program_id(0) == 1)
    def _():
        fetch.wait()
        for copy in copies:
            copy.start()

    width = CZ * TILE
    column = lax.broadcasted_iota(jnp.int32, (TILE, width), 1) % TILE
    agree = column == lax.broadcasted_iota(jnp.int32, (TILE, width), 0)
    place = lax.broadcasted_iota(jnp.int32, (width, LANES), 0) // TILE
    gather = place == lax.broadcasted_iota(jnp.int32, (width, LANES), 1)
    gather = jnp.where(gather, 1.0, 0.0).astype(jnp.bfloat16)
    upper = lax.broadcasted_iota(jnp.int32, (2 * TILE, CHUNK), 0) // TILE
    upper = upper.astype(jnp.float32)
    one = jnp.ones((2 * TILE, CHUNK), jnp.bfloat16)
    nil = jnp.zeros((2 * TILE, CHUNK), jnp.bfloat16)

    for r in range(OY):

        def body(j, total):
            at = pl.ds(pl.multiple_of(j * CHUNK, CHUNK), CHUNK)
            cell = jnp.where(fluid_ref[r, :, at] > 0, ids_ref[r, :, at], -1).astype(jnp.float32)
            cell = (jnp.concatenate([cell, cell], 0) - upper).astype(jnp.bfloat16)
            hits = [jnp.where(cell == jnp.bfloat16(k), one, nil) for k in range(0, CZ, 2)]
            terms = in_bfloat16(jnp.concatenate([vel_ref[c, r, :, at] for c in range(3)], 0))
            terms.append(jnp.ones((TILE, CHUNK), jnp.float32))
            terms = jnp.concatenate(terms, 0).astype(jnp.bfloat16)
            return total + product(terms, jnp.concatenate(hits, 0), 1)

        total = jnp.zeros((10 * TILE, width), jnp.float32)
        total = lax.fori_loop(0, atoms // CHUNK, body, total)
        sums = total[: 3 * TILE] + total[3 * TILE : 6 * TILE] + total[6 * TILE : 9 * TILE]
        parts = [sums[c * TILE : (c + 1) * TILE] for c in range(3)] + [total[9 * TILE :]]
        parts = jnp.concatenate([jnp.where(agree, part, 0.0) for part in parts], 0)
        found = product(jnp.concatenate(in_bfloat16(parts), 0).astype(jnp.bfloat16), gather, 0)
        found = found[: 4 * TILE] + found[4 * TILE : 8 * TILE] + found[8 * TILE :]
        count = found[3 * TILE :]
        divisor = jnp.maximum(count, 1.0)
        out = pltpu.roll(count, 3 * CZ, 1)
        for c in range(3):
            mean = found[c * TILE : (c + 1) * TILE] / divisor
            out = out + (pltpu.roll(mean, c * CZ, 1) if c else mean)
        out_ref[:, pl.ds(r * LANES, LANES)] = out
        for x in range(TILE):
            send_ref[x // 2, pl.ds((x % 2) * OY + r, 1), :] = out[x : x + 1]
            send_ref[x // 2, pl.ds(4 + (x % 2) * OY + r, 1), :] = out[x : x + 1]

    @pl.when(pl.program_id(0) == pl.num_programs(0) - 1)
    def _():
        for copy in copies:
            copy.wait()


def cell_means(vel, ids, fluid, field, cuts):
    _, _, nx, atoms = vel.shape
    assert nx >= 2 * TILE and atoms % CHUNK == 0
    atom_block = pl.BlockSpec((OY, TILE, atoms), lambda x: (0, x, 0))
    return pl.pallas_call(
        functools.partial(means_kernel, atoms=atoms, cuts=cuts),
        grid=(nx // TILE,),
        in_specs=[
            pl.BlockSpec((3, OY, TILE, atoms), lambda x: (0, 0, x, 0)),
            atom_block,
            atom_block,
            pl.BlockSpec(memory_space=pltpu.HBM),
        ],
        out_specs=[
            pl.BlockSpec((TILE, OY * LANES), lambda x: (x, 0)),
            pl.BlockSpec((TILE // 2, 8, LANES), lambda x: (x, 0, 0)),
        ]
        + [pl.BlockSpec(memory_space=pltpu.HBM)] * (len(cuts) - 1),
        out_shape=[
            jax.ShapeDtypeStruct((nx, OY * LANES), jnp.float32),
            jax.ShapeDtypeStruct((nx // 2, 8, LANES), jnp.float32),
        ]
        + [
            jax.ShapeDtypeStruct((3, 2, b - a, field.shape[3]), jnp.float32)
            for a, b in zip(cuts[:-1], cuts[1:])
        ],
        scratch_shapes=[
            pltpu.VMEM((3, 2, cuts[-1] - cuts[0], field.shape[3]), jnp.float32),
            pltpu.SemaphoreType.DMA((len(cuts),)),
        ],
        compiler_params=pltpu.CompilerParams(vmem_limit_bytes=VMEM_BYTES),
        cost_estimate=pl.CostEstimate(flops=10**8, bytes_accessed=40 * 10**6, transcendentals=0),
        name="cell_means",
    )(vel, ids, fluid, field)


def spread(block, k):
    return pltpu.roll(block, k % 4 * CZ, 1) if k % 4 else block


def seed_kernel(slab_ref, field_ref, out_ref):
    lane = lax.broadcasted_iota(jnp.int32, (TILE, LANES), 1) // CZ
    source = lax.broadcasted_iota(jnp.int32, (TILE, LANES), 0) // 2
    for q in range(slab_ref.shape[0] // 4):
        at = pl.ds(q * LANES, LANES)
        for r in range(OY):
            rows = [slab_ref[4 * q + m, pl.ds(p * OY + r, 1), :] for m in range(4) for p in range(2)]
            block = jnp.concatenate(rows, 0)
            turned = [spread(block, k) for k in range(4)]
            whole = []
            for c in range(4):
                part = jnp.zeros((TILE, LANES), jnp.float32)
                for m in range(4):
                    mine = jnp.logical_and(source == m, lane == m)
                    part = jnp.where(mine, turned[(m - c) % 4], part)
                part = part + pltpu.roll(part, 4, 0)
                whole.append(part + pltpu.roll(part, 2, 0))
            for c in range(3):
                for p in range(2):
                    kept = field_ref[c, p, pl.ds(r, 1), at]
                    fresh = jnp.where(whole[3][p : p + 1] > 0, whole[c][p : p + 1], kept)
                    out_ref[c, p, pl.ds(r, 1), at] = fresh
    out_ref[:, :, pl.ds(OY, LOW - OY), :] = field_ref[:, :, pl.ds(OY, LOW - OY), :]


def seed(slab, field):
    block = pl.BlockSpec((3, 2, LOW, field.shape[3]), lambda i: (0, 0, 0, 0))
    return pl.pallas_call(
        seed_kernel,
        grid=(1,),
        in_specs=[pl.BlockSpec(slab.shape, lambda i: (0, 0, 0)), block],
        out_specs=block,
        out_shape=jax.ShapeDtypeStruct((3, 2, LOW, field.shape[3]), jnp.float32),
        compiler_params=pltpu.CompilerParams(vmem_limit_bytes=VMEM_BYTES),
        name="seed",
    )(slab, field)


def write_back(low_ref, out_ref):
    lane = lax.broadcasted_iota(jnp.int32, (TILE, LANES), 1) // CZ
    row = lax.broadcasted_iota(jnp.int32, (TILE, LANES), 0)
    for q in range(out_ref.shape[0] // 4):
        at = pl.ds(q * LANES, LANES)
        for r in range(OY):
            block = jnp.zeros((TILE, LANES), jnp.float32)
            for c in range(3):
                even, odd = (low_ref[c, p, pl.ds(r, 1), at] for p in range(2))
                both = jnp.where(row % 2 == 0, even, odd)
                for m in range(4):
                    mine = jnp.logical_and(row // 2 == m, lane == c)
                    block = jnp.where(mine, spread(both, c - m), block)
            for m in range(4):
                for p in range(2):
                    line = block[2 * m + p : 2 * m + p + 1]
                    out_ref[4 * q + m, pl.ds(p * OY + r, 1), :] = line
                    out_ref[4 * q + m, pl.ds(4 + p * OY + r, 1), :] = line


def constrain_kernel(vel_ref, ids_ref, fluid_ref, new_ref, mean_ref, out_ref, *, atoms):
    for r in range(OY):
        rows = [new_ref[x // 2, pl.ds((x % 2) * OY + r, 1), :] for x in range(TILE)]
        delta = jnp.concatenate(rows, 0) - mean_ref[:, pl.ds(r * LANES, LANES)]
        for j in range(atoms // LANES):
            at = pl.ds(j * LANES, LANES)
            cell = ids_ref[r, :, at]
            weight = fluid_ref[r, :, at].astype(jnp.float32)
            for c in range(3):
                step = jnp.take_along_axis(delta, cell + c * CZ, axis=1)
                out_ref[c, r, :, at] = vel_ref[c, r, :, at] + weight * step


def constrain(vel, ids, fluid, new, mean):
    _, _, nx, atoms = vel.shape
    vel_block = pl.BlockSpec((3, OY, TILE, atoms), lambda x: (0, 0, x, 0))
    atom_block = pl.BlockSpec((OY, TILE, atoms), lambda x: (0, x, 0))
    return pl.pallas_call(
        functools.partial(constrain_kernel, atoms=atoms),
        grid=(nx // TILE,),
        in_specs=[
            vel_block,
            atom_block,
            atom_block,
            pl.BlockSpec((TILE // 2, 8, LANES), lambda x: (x, 0, 0)),
            pl.BlockSpec((TILE, OY * LANES), lambda x: (x, 0)),
        ],
        out_specs=vel_block,
        out_shape=jax.ShapeDtypeStruct(vel.shape, vel.dtype),
        compiler_params=pltpu.CompilerParams(vmem_limit_bytes=VMEM_BYTES),
        cost_estimate=pl.CostEstimate(flops=10**7, bytes_accessed=20 * 10**6, transcendentals=0),
        name="constrain",
    )(vel, ids, fluid, new, mean)


def plane_update(read, below, above, plane):
    centre = [read(c, plane) for c in range(3)]
    speed = [COURANT * u for u in centre]
    ahead = [VISCOUS - s for s in speed]
    behind = [VISCOUS + s for s in speed]
    nz = centre[0].shape[-1]
    fresh = []
    for c in range(3):
        u = centre[c]
        along_x = read(c, plane + 1) * ahead[0] + read(c, plane - 1) * behind[0]
        along_y = above(c, plane, u) * ahead[1] + below(c, plane, u) * behind[1]
        along_z = pltpu.roll(u, nz - 1, 1) * ahead[2] + pltpu.roll(u, 1, 1) * behind[2]
        fresh.append((1.0 - 6.0 * VISCOUS) * u + along_x + (along_y + along_z))
    return fresh


def two_steps_kernel(*refs, copies, segments, lo, hi, ny, n_in, low_rows):
    core_ref, ins, out_ref = refs[0], refs[1 : n_in + 1], refs[n_in + 1]
    start_ref, step_ref, new_ref, in_sem, out_sem = refs[-5:]
    tiles = (hi - lo) // TILE
    nz = start_ref.shape[-1]
    place = {"own": 2, "chip": 4 - 4 * core_ref[0], "far": 4 * core_ref[0]}

    pending = {}
    for number, (segment, source, plane, at, to, count) in enumerate(copies):
        copy = pltpu.make_async_copy(
            ins[source].at[:, :, pl.ds(at, count), :],
            start_ref.at[:, pl.ds(place[plane], 2), pl.ds(to, count), :],
            in_sem.at[number],
        )
        copy.start()
        pending.setdefault(segment, []).append(copy)
    outgoing = []
    if low_rows is not None:
        outgoing.append(
            pltpu.make_async_copy(
                ins[low_rows], out_ref.at[:, :, pl.ds(0, TILE), :], out_sem.at[0]
            )
        )
        outgoing[0].start()

    if lo == 0:
        for ref, planes in ((start_ref, 6), (step_ref, 4)):
            ref[:, :, pl.ds(TILE, TILE), :] = jnp.zeros((3, planes, TILE, nz), jnp.float32)
    if hi == ny:
        for ref, planes in ((start_ref, 6), (step_ref, 4)):
            at = pl.ds((tiles + 2) * TILE, TILE)
            ref[0, :, at, :] = jnp.full((planes, TILE, nz), PLATE_SPEED, jnp.float32)
            ref[1:, :, at, :] = jnp.zeros((2, planes, TILE, nz), jnp.float32)

    row = lax.broadcasted_iota(jnp.int32, (TILE, nz), 0)

    def readers(ref, t):
        def tile(c, plane, step):
            at = pl.ds(pl.multiple_of((t + step) * TILE, TILE), TILE)
            return ref[c, plane, at, :]

        def read(c, plane):
            return tile(c, plane, 0)

        def below(c, plane, u):
            return pltpu.roll(jnp.where(row == TILE - 1, tile(c, plane, -1), u), 1, 0)

        def above(c, plane, u):
            return pltpu.roll(jnp.where(row == 0, tile(c, plane, 1), u), TILE - 1, 0)

        return read, below, above

    def first_step(t):
        read, below, above = readers(start_ref, t)
        for plane in range(4):
            fresh = plane_update(read, below, above, plane + 1)
            for c in range(3):
                step_ref[c, plane, pl.ds(pl.multiple_of(t * TILE, TILE), TILE), :] = fresh[c]

    def second_step(t):
        read, below, above = readers(step_ref, t)
        for plane in range(2):
            fresh = plane_update(read, below, above, plane + 1)
            for c in range(3):
                at = pl.ds(pl.multiple_of((t - 2) * TILE, TILE), TILE)
                new_ref[c, plane, at, :] = fresh[c]

    def both_steps(t, carry):
        first_step(t)
        second_step(t - 1)
        return carry

    done_first, done_second = (1 if lo == 0 else 0), 1
    for segment, last_tile in enumerate(segments):
        for copy in pending.get(segment, []):
            copy.wait()
        end_first = tiles + 1 if hi == ny else tiles + 2
        reach_first = min(last_tile - 1, end_first) if segment < len(segments) - 1 else end_first
        reach_second = min(reach_first - 1, tiles + 1)
        while done_first < reach_first and done_second >= done_first:
            done_first += 1
            first_step(done_first)
        head = done_second
        if done_first == done_second + 1:
            begin = done_first + 1
        else:
            while done_first < min(reach_first, done_second + 1):
                done_first += 1
                first_step(done_first)
            begin = done_first + 1
        if reach_first >= begin:
            lax.fori_loop(begin, reach_first + 1, both_steps, 0)
            done_first = reach_first
            done_second = max(done_second, reach_first - 1)
        if segment == len(segments) - 1:
            while done_second < tiles + 1:
                done_second += 1
                second_step(done_second)
        if done_second > head:
            at, count = (head - 1) * TILE, (done_second - head) * TILE
            copy = pltpu.make_async_copy(
                new_ref.at[:, :, pl.ds(at, count), :],
                out_ref.at[:, :, pl.ds(at + (lo if out_ref.shape[2] == ny else 0), count), :],
                out_sem.at[len(outgoing)],
            )
            copy.start()
            outgoing.append(copy)
    if lo == 0:
        write_back(new_ref, refs[n_in + 2])
    for copy in outgoing:
        copy.wait()


def two_steps(core, own, chip, far, lo, hi, ny, cuts=(), into=None, low=None, whole=True):
    nz = own[0][0].shape[-1]
    ins, copies = [], []
    floor, ceiling = max(lo - TILE, 0), min(hi + TILE, ny)
    edges = [floor] + [cut for cut in cuts if floor < cut < ceiling] + [ceiling]
    for plane, pieces in (("own", own), ("chip", chip), ("far", far)):
        for array, first, *least in pieces:
            last = first + array.shape[2]
            used = False
            for segment, (a, b) in enumerate(zip(edges[:-1], edges[1:])):
                a, b = max(a, first, *least), min(b, last)
                if a < b:
                    copies.append(
                        (segment, len(ins), plane, a - first, a - lo + 2 * TILE, b - a)
                    )
                    used = True
            if used:
                ins.append(array)
    segments = [(edge - lo) // TILE + 1 for edge in edges[1:]]
    low_rows = None
    if low is not None:
        low_rows = len(ins)
        ins.append(low)
    aliases = {}
    if into is not None:
        aliases = {len(ins) + 1: 0}
        ins.append(into)
    copies.sort(key=lambda copy: copy[0])
    span = hi - lo
    anywhere = pl.BlockSpec(memory_space=pltpu.HBM)
    return pl.pallas_call(
        functools.partial(
            two_steps_kernel,
            copies=copies,
            segments=segments,
            lo=lo,
            hi=hi,
            ny=ny,
            n_in=len(ins),
            low_rows=low_rows,
        ),
        in_specs=[pl.BlockSpec(memory_space=pltpu.SMEM)] + [anywhere] * len(ins),
        out_specs=[anywhere] + [pl.BlockSpec(memory_space=pltpu.VMEM)] * (lo == 0),
        out_shape=[
            jax.ShapeDtypeStruct((3, 2, ny if whole else span, nz), jnp.float32),
            jax.ShapeDtypeStruct((nz // CZ, 8, LANES), jnp.float32),
        ][: 1 + (lo == 0)],
        scratch_shapes=[
            pltpu.VMEM((3, 6, span + 4 * TILE, nz), jnp.float32),
            pltpu.VMEM((3, 4, span + 4 * TILE, nz), jnp.float32),
            pltpu.VMEM((3, 2, span, nz), jnp.float32),
            pltpu.SemaphoreType.DMA((len(copies),)),
            pltpu.SemaphoreType.DMA((len(segments) + 1,)),
        ],
        input_output_aliases=aliases,
        compiler_params=pltpu.CompilerParams(vmem_limit_bytes=VMEM_BYTES),
        cost_estimate=pl.CostEstimate(
            flops=span * 10**6, bytes_accessed=span * 60 * 10**3, transcendentals=0
        ),
        name="two_steps",
    )(core, *ins)


def tie(value, *others):
    return lax.optimization_barrier((value,) + others)[0]


def local(field, atom_vel, cell_ids, fluid):
    ny = field.shape[2]
    count = lax.axis_size("gx") * lax.axis_size("gz")
    core = (lax.axis_index("gz") % 2).reshape(1)
    chip_pairs, far_pairs = [], []
    for i in range(0, count, 2):
        chip_pairs += [(i, i + 1), (i + 1, i)]
        far_pairs += [(i + 1, (i + 2) % count), ((i + 2) % count, i + 1)]

    def over_chip(block):
        return lax.ppermute(block, ROW_AXES, chip_pairs)

    def over_links(block):
        return lax.ppermute(block, ROW_AXES, far_pairs)

    def exchange(block):
        return lax.all_to_all(block, "gz", split_axis=0, concat_axis=0, tiled=True)

    first = over_links(field[:, :, LOW:FIRST])
    chip = over_chip(field)
    means, outgoing, *blocks = cell_means(
        atom_vel, cell_ids, fluid, field, (FIRST, SECOND, ny)
    )
    slab = exchange(outgoing)
    base = seed(slab, field)
    base_chip, base_far = over_chip(base), over_links(base)
    second = over_links(tie(blocks[0], base_chip, base_far, first, chip))
    low, returned = two_steps(
        core,
        [(base, 0), (field, 0, LOW)],
        [(base_chip, 0), (chip, 0, LOW)],
        [(base_far, 0), (first, LOW)],
        0,
        TILE,
        ny,
        whole=False,
    )
    back = exchange(returned)
    own, beside = [(field, 0)], [(chip, 0)]
    far = [(base_far, 0), (first, LOW), (second, FIRST)]
    third = over_links(tie(blocks[1], second, back))
    far.append((third, SECOND))
    new_atoms = constrain(atom_vel, cell_ids, fluid, back, means)
    start, reach = TILE, SECOND - TILE
    (part,) = two_steps(core, own, beside, far[:3], start, reach, ny, (40, 72, 104, 136))
    (new_field,) = two_steps(
        core, own, beside, far[2:], reach, ny, ny, (208, 232), into=part, low=low
    )
    return new_field, new_atoms


def solution(mesh):
    placed = (
        P(None, ("gx", "gz"), None, None),
        P(None, None, "gx", "gz"),
        P(None, "gx", "gz"),
        P(None, "gx", "gz"),
    )
    return jax.shard_map(
        local,
        mesh=mesh,
        in_specs=placed,
        out_specs=(P(None, ("gx", "gz"), None, None), P(None, None, "gx", "gz")),
        check_vma=False,
    )
```

```python
import functools

import jax
import jax.numpy as jnp
from jax import lax
from jax.experimental import pallas as pl
from jax.experimental.pallas import tpu as pltpu
from jax.sharding import PartitionSpec as P

CZ = 32
OY = 2
LANES = 128
TILE = 8
CHUNK = 2048
VMEM_BYTES = 64 * 2**20
LOW = 8
FIRST = 104
SECOND = 184

VISCOUS = 0.15
COURANT = 0.05
PLATE_SPEED = 1.0

ROW_AXES = ("gx", "gz")


def product(a, b, contract):
    return lax.dot_general(
        a, b, (((1,), (contract,)), ((), ())), preferred_element_type=jnp.float32
    )


def in_bfloat16(values):
    terms = []
    for _ in range(3):
        terms.append(values.astype(jnp.bfloat16).astype(jnp.float32))
        values = values - terms[-1]
    return terms


def means_kernel(vel_ref, ids_ref, fluid_ref, field_ref, out_ref, send_ref, *refs, atoms, cuts):
    pieces, (held_ref, sem) = refs[:-2], refs[-2:]
    fetch = pltpu.make_async_copy(
        field_ref.at[:, :, pl.ds(cuts[0], cuts[-1] - cuts[0]), :], held_ref, sem.at[len(pieces)]
    )
    copies = [
        pltpu.make_async_copy(
            held_ref.at[:, :, pl.ds(a - cuts[0], b - a), :], piece, sem.at[number]
        )
        for number, (a, b, piece) in enumerate(zip(cuts[:-1], cuts[1:], pieces))
    ]

    @pl.when(pl.program_id(0) == 0)
    def _():
        fetch.start()

    @pl.when(pl.program_id(0) == 1)
    def _():
        fetch.wait()
        for copy in copies:
            copy.start()

    width = CZ * TILE
    column = lax.broadcasted_iota(jnp.int32, (TILE, width), 1) % TILE
    agree = column == lax.broadcasted_iota(jnp.int32, (TILE, width), 0)
    place = lax.broadcasted_iota(jnp.int32, (width, LANES), 0) // TILE
    gather = place == lax.broadcasted_iota(jnp.int32, (width, LANES), 1)
    gather = jnp.where(gather, 1.0, 0.0).astype(jnp.bfloat16)
    upper = lax.broadcasted_iota(jnp.int32, (2 * TILE, CHUNK), 0) // TILE
    upper = upper.astype(jnp.float32)
    one = jnp.ones((2 * TILE, CHUNK), jnp.bfloat16)
    nil = jnp.zeros((2 * TILE, CHUNK), jnp.bfloat16)

    for r in range(OY):

        def body(j, total):
            at = pl.ds(pl.multiple_of(j * CHUNK, CHUNK), CHUNK)
            cell = jnp.where(fluid_ref[r, :, at] > 0, ids_ref[r, :, at], -1).astype(jnp.float32)
            cell = (jnp.concatenate([cell, cell], 0) - upper).astype(jnp.bfloat16)
            hits = [jnp.where(cell == jnp.bfloat16(k), one, nil) for k in range(0, CZ, 2)]
            terms = in_bfloat16(jnp.concatenate([vel_ref[c, r, :, at] for c in range(3)], 0))
            terms.append(jnp.ones((TILE, CHUNK), jnp.float32))
            terms = jnp.concatenate(terms, 0).astype(jnp.bfloat16)
            return total + product(terms, jnp.concatenate(hits, 0), 1)

        total = jnp.zeros((10 * TILE, width), jnp.float32)
        total = lax.fori_loop(0, atoms // CHUNK, body, total)
        sums = total[: 3 * TILE] + total[3 * TILE : 6 * TILE] + total[6 * TILE : 9 * TILE]
        parts = [sums[c * TILE : (c + 1) * TILE] for c in range(3)] + [total[9 * TILE :]]
        parts = jnp.concatenate([jnp.where(agree, part, 0.0) for part in parts], 0)
        found = product(jnp.concatenate(in_bfloat16(parts), 0).astype(jnp.bfloat16), gather, 0)
        found = found[: 4 * TILE] + found[4 * TILE : 8 * TILE] + found[8 * TILE :]
        count = found[3 * TILE :]
        divisor = jnp.maximum(count, 1.0)
        out = pltpu.roll(count, 3 * CZ, 1)
        for c in range(3):
            mean = found[c * TILE : (c + 1) * TILE] / divisor
            out = out + (pltpu.roll(mean, c * CZ, 1) if c else mean)
        out_ref[:, pl.ds(r * LANES, LANES)] = out
        for x in range(TILE):
            send_ref[x // 2, pl.ds((x % 2) * OY + r, 1), :] = out[x : x + 1]

    @pl.when(pl.program_id(0) == pl.num_programs(0) - 1)
    def _():
        for copy in copies:
            copy.wait()


def cell_means(vel, ids, fluid, field, cuts):
    _, _, nx, atoms = vel.shape
    assert nx >= 2 * TILE and atoms % CHUNK == 0
    atom_block = pl.BlockSpec((OY, TILE, atoms), lambda x: (0, x, 0))
    return pl.pallas_call(
        functools.partial(means_kernel, atoms=atoms, cuts=cuts),
        grid=(nx // TILE,),
        in_specs=[
            pl.BlockSpec((3, OY, TILE, atoms), lambda x: (0, 0, x, 0)),
            atom_block,
            atom_block,
            pl.BlockSpec(memory_space=pltpu.HBM),
        ],
        out_specs=[
            pl.BlockSpec((TILE, OY * LANES), lambda x: (x, 0)),
            pl.BlockSpec((TILE // 2, 2 * OY, LANES), lambda x: (x, 0, 0)),
        ]
        + [pl.BlockSpec(memory_space=pltpu.HBM)] * (len(cuts) - 1),
        out_shape=[
            jax.ShapeDtypeStruct((nx, OY * LANES), jnp.float32),
            jax.ShapeDtypeStruct((nx // 2, 2 * OY, LANES), jnp.float32),
        ]
        + [
            jax.ShapeDtypeStruct((3, 2, b - a, field.shape[3]), jnp.float32)
            for a, b in zip(cuts[:-1], cuts[1:])
        ],
        scratch_shapes=[
            pltpu.VMEM((3, 2, cuts[-1] - cuts[0], field.shape[3]), jnp.float32),
            pltpu.SemaphoreType.DMA((len(cuts),)),
        ],
        compiler_params=pltpu.CompilerParams(vmem_limit_bytes=VMEM_BYTES),
        cost_estimate=pl.CostEstimate(flops=10**8, bytes_accessed=40 * 10**6, transcendentals=0),
        name="cell_means",
    )(vel, ids, fluid, field)


def spread(block, k):
    return pltpu.roll(block, k % 4 * CZ, 1) if k % 4 else block


def seed_kernel(slab_ref, field_ref, out_ref):
    lane = lax.broadcasted_iota(jnp.int32, (TILE, LANES), 1) // CZ
    source = lax.broadcasted_iota(jnp.int32, (TILE, LANES), 0) // 2
    for q in range(slab_ref.shape[0] // 4):
        at = pl.ds(q * LANES, LANES)
        for r in range(OY):
            rows = [slab_ref[4 * q + m, pl.ds(p * OY + r, 1), :] for m in range(4) for p in range(2)]
            block = jnp.concatenate(rows, 0)
            turned = [spread(block, k) for k in range(4)]
            whole = []
            for c in range(4):
                part = jnp.zeros((TILE, LANES), jnp.float32)
                for m in range(4):
                    mine = jnp.logical_and(source == m, lane == m)
                    part = jnp.where(mine, turned[(m - c) % 4], part)
                part = part + pltpu.roll(part, 4, 0)
                whole.append(part + pltpu.roll(part, 2, 0))
            for c in range(3):
                for p in range(2):
                    kept = field_ref[c, p, pl.ds(r, 1), at]
                    fresh = jnp.where(whole[3][p : p + 1] > 0, whole[c][p : p + 1], kept)
                    out_ref[c, p, pl.ds(r, 1), at] = fresh
    out_ref[:, :, pl.ds(OY, LOW - OY), :] = field_ref[:, :, pl.ds(OY, LOW - OY), :]


def seed(slab, field):
    block = pl.BlockSpec((3, 2, LOW, field.shape[3]), lambda i: (0, 0, 0, 0))
    return pl.pallas_call(
        seed_kernel,
        grid=(1,),
        in_specs=[pl.BlockSpec(slab.shape, lambda i: (0, 0, 0)), block],
        out_specs=block,
        out_shape=jax.ShapeDtypeStruct((3, 2, LOW, field.shape[3]), jnp.float32),
        compiler_params=pltpu.CompilerParams(vmem_limit_bytes=VMEM_BYTES),
        name="seed",
    )(slab, field)


def write_back(low_ref, out_ref):
    lane = lax.broadcasted_iota(jnp.int32, (TILE, LANES), 1) // CZ
    row = lax.broadcasted_iota(jnp.int32, (TILE, LANES), 0)
    for q in range(out_ref.shape[0] // 4):
        at = pl.ds(q * LANES, LANES)
        for r in range(OY):
            block = jnp.zeros((TILE, LANES), jnp.float32)
            for c in range(3):
                even, odd = (low_ref[c, p, pl.ds(r, 1), at] for p in range(2))
                both = jnp.where(row % 2 == 0, even, odd)
                for m in range(4):
                    mine = jnp.logical_and(row // 2 == m, lane == c)
                    block = jnp.where(mine, spread(both, c - m), block)
            for m in range(4):
                for p in range(2):
                    line = block[2 * m + p : 2 * m + p + 1]
                    out_ref[4 * q + m, pl.ds(p * OY + r, 1), :] = line


def constrain_kernel(vel_ref, ids_ref, fluid_ref, new_ref, mean_ref, out_ref, *, atoms):
    for r in range(OY):
        rows = [new_ref[x // 2, pl.ds((x % 2) * OY + r, 1), :] for x in range(TILE)]
        delta = jnp.concatenate(rows, 0) - mean_ref[:, pl.ds(r * LANES, LANES)]
        for j in range(atoms // LANES):
            at = pl.ds(j * LANES, LANES)
            cell = ids_ref[r, :, at]
            weight = fluid_ref[r, :, at].astype(jnp.float32)
            for c in range(3):
                step = jnp.take_along_axis(delta, cell + c * CZ, axis=1)
                out_ref[c, r, :, at] = vel_ref[c, r, :, at] + weight * step


def constrain(vel, ids, fluid, new, mean):
    _, _, nx, atoms = vel.shape
    vel_block = pl.BlockSpec((3, OY, TILE, atoms), lambda x: (0, 0, x, 0))
    atom_block = pl.BlockSpec((OY, TILE, atoms), lambda x: (0, x, 0))
    return pl.pallas_call(
        functools.partial(constrain_kernel, atoms=atoms),
        grid=(nx // TILE,),
        in_specs=[
            vel_block,
            atom_block,
            atom_block,
            pl.BlockSpec((TILE // 2, 2 * OY, LANES), lambda x: (x, 0, 0)),
            pl.BlockSpec((TILE, OY * LANES), lambda x: (x, 0)),
        ],
        out_specs=vel_block,
        out_shape=jax.ShapeDtypeStruct(vel.shape, vel.dtype),
        compiler_params=pltpu.CompilerParams(vmem_limit_bytes=VMEM_BYTES),
        cost_estimate=pl.CostEstimate(flops=10**7, bytes_accessed=20 * 10**6, transcendentals=0),
        name="constrain",
    )(vel, ids, fluid, new, mean)


def plane_update(read, below, above, plane):
    centre = [read(c, plane) for c in range(3)]
    speed = [COURANT * u for u in centre]
    ahead = [VISCOUS - s for s in speed]
    behind = [VISCOUS + s for s in speed]
    nz = centre[0].shape[-1]
    fresh = []
    for c in range(3):
        u = centre[c]
        along_x = read(c, plane + 1) * ahead[0] + read(c, plane - 1) * behind[0]
        along_y = above(c, plane, u) * ahead[1] + below(c, plane, u) * behind[1]
        along_z = pltpu.roll(u, nz - 1, 1) * ahead[2] + pltpu.roll(u, 1, 1) * behind[2]
        fresh.append((1.0 - 6.0 * VISCOUS) * u + along_x + (along_y + along_z))
    return fresh


def two_steps_kernel(*refs, copies, segments, lo, hi, ny, n_in, low_rows):
    core_ref, ins, out_ref = refs[0], refs[1 : n_in + 1], refs[n_in + 1]
    start_ref, step_ref, new_ref, in_sem, out_sem = refs[-5:]
    tiles = (hi - lo) // TILE
    nz = start_ref.shape[-1]
    place = {"own": 2, "chip": 4 - 4 * core_ref[0], "far": 4 * core_ref[0]}

    pending = {}
    for number, (segment, source, plane, at, to, count) in enumerate(copies):
        copy = pltpu.make_async_copy(
            ins[source].at[:, :, pl.ds(at, count), :],
            start_ref.at[:, pl.ds(place[plane], 2), pl.ds(to, count), :],
            in_sem.at[number],
        )
        copy.start()
        pending.setdefault(segment, []).append(copy)
    outgoing = []
    if low_rows is not None:
        outgoing.append(
            pltpu.make_async_copy(
                ins[low_rows], out_ref.at[:, :, pl.ds(0, TILE), :], out_sem.at[0]
            )
        )
        outgoing[0].start()

    if lo == 0:
        for ref, planes in ((start_ref, 6), (step_ref, 4)):
            ref[:, :, pl.ds(TILE, TILE), :] = jnp.zeros((3, planes, TILE, nz), jnp.float32)
    if hi == ny:
        for ref, planes in ((start_ref, 6), (step_ref, 4)):
            at = pl.ds((tiles + 2) * TILE, TILE)
            ref[0, :, at, :] = jnp.full((planes, TILE, nz), PLATE_SPEED, jnp.float32)
            ref[1:, :, at, :] = jnp.zeros((2, planes, TILE, nz), jnp.float32)

    row = lax.broadcasted_iota(jnp.int32, (TILE, nz), 0)

    def readers(ref, t):
        def tile(c, plane, step):
            at = pl.ds(pl.multiple_of((t + step) * TILE, TILE), TILE)
            return ref[c, plane, at, :]

        def read(c, plane):
            return tile(c, plane, 0)

        def below(c, plane, u):
            return pltpu.roll(jnp.where(row == TILE - 1, tile(c, plane, -1), u), 1, 0)

        def above(c, plane, u):
            return pltpu.roll(jnp.where(row == 0, tile(c, plane, 1), u), TILE - 1, 0)

        return read, below, above

    def first_step(t):
        read, below, above = readers(start_ref, t)
        for plane in range(4):
            fresh = plane_update(read, below, above, plane + 1)
            for c in range(3):
                step_ref[c, plane, pl.ds(pl.multiple_of(t * TILE, TILE), TILE), :] = fresh[c]

    def second_step(t):
        read, below, above = readers(step_ref, t)
        for plane in range(2):
            fresh = plane_update(read, below, above, plane + 1)
            for c in range(3):
                at = pl.ds(pl.multiple_of((t - 2) * TILE, TILE), TILE)
                new_ref[c, plane, at, :] = fresh[c]

    def both_steps(t, carry):
        first_step(t)
        second_step(t - 1)
        return carry

    done_first, done_second = (1 if lo == 0 else 0), 1
    for segment, last_tile in enumerate(segments):
        for copy in pending.get(segment, []):
            copy.wait()
        end_first = tiles + 1 if hi == ny else tiles + 2
        reach_first = min(last_tile - 1, end_first) if segment < len(segments) - 1 else end_first
        reach_second = min(reach_first - 1, tiles + 1)
        while done_first < reach_first and done_second >= done_first:
            done_first += 1
            first_step(done_first)
        head = done_second
        if done_first == done_second + 1:
            begin = done_first + 1
        else:
            while done_first < min(reach_first, done_second + 1):
                done_first += 1
                first_step(done_first)
            begin = done_first + 1
        if reach_first >= begin:
            lax.fori_loop(begin, reach_first + 1, both_steps, 0)
            done_first = reach_first
            done_second = max(done_second, reach_first - 1)
        if segment == len(segments) - 1:
            while done_second < tiles + 1:
                done_second += 1
                second_step(done_second)
        if done_second > head:
            at, count = (head - 1) * TILE, (done_second - head) * TILE
            copy = pltpu.make_async_copy(
                new_ref.at[:, :, pl.ds(at, count), :],
                out_ref.at[:, :, pl.ds(at + (lo if out_ref.shape[2] == ny else 0), count), :],
                out_sem.at[len(outgoing)],
            )
            copy.start()
            outgoing.append(copy)
    if lo == 0:
        write_back(new_ref, refs[n_in + 2])
    for copy in outgoing:
        copy.wait()


def two_steps(core, own, chip, far, lo, hi, ny, cuts=(), into=None, low=None, whole=True):
    nz = own[0][0].shape[-1]
    ins, copies = [], []
    floor, ceiling = max(lo - TILE, 0), min(hi + TILE, ny)
    edges = [floor] + [cut for cut in cuts if floor < cut < ceiling] + [ceiling]
    for plane, pieces in (("own", own), ("chip", chip), ("far", far)):
        for array, first, *least in pieces:
            last = first + array.shape[2]
            used = False
            for segment, (a, b) in enumerate(zip(edges[:-1], edges[1:])):
                a, b = max(a, first, *least), min(b, last)
                if a < b:
                    copies.append(
                        (segment, len(ins), plane, a - first, a - lo + 2 * TILE, b - a)
                    )
                    used = True
            if used:
                ins.append(array)
    segments = [(edge - lo) // TILE + 1 for edge in edges[1:]]
    low_rows = None
    if low is not None:
        low_rows = len(ins)
        ins.append(low)
    aliases = {}
    if into is not None:
        aliases = {len(ins) + 1: 0}
        ins.append(into)
    copies.sort(key=lambda copy: copy[0])
    span = hi - lo
    anywhere = pl.BlockSpec(memory_space=pltpu.HBM)
    return pl.pallas_call(
        functools.partial(
            two_steps_kernel,
            copies=copies,
            segments=segments,
            lo=lo,
            hi=hi,
            ny=ny,
            n_in=len(ins),
            low_rows=low_rows,
        ),
        in_specs=[pl.BlockSpec(memory_space=pltpu.SMEM)] + [anywhere] * len(ins),
        out_specs=[anywhere] + [pl.BlockSpec(memory_space=pltpu.VMEM)] * (lo == 0),
        out_shape=[
            jax.ShapeDtypeStruct((3, 2, ny if whole else span, nz), jnp.float32),
            jax.ShapeDtypeStruct((nz // CZ, 2 * OY, LANES), jnp.float32),
        ][: 1 + (lo == 0)],
        scratch_shapes=[
            pltpu.VMEM((3, 6, span + 4 * TILE, nz), jnp.float32),
            pltpu.VMEM((3, 4, span + 4 * TILE, nz), jnp.float32),
            pltpu.VMEM((3, 2, span, nz), jnp.float32),
            pltpu.SemaphoreType.DMA((len(copies),)),
            pltpu.SemaphoreType.DMA((len(segments) + 1,)),
        ],
        input_output_aliases=aliases,
        compiler_params=pltpu.CompilerParams(vmem_limit_bytes=VMEM_BYTES),
        cost_estimate=pl.CostEstimate(
            flops=span * 10**6, bytes_accessed=span * 60 * 10**3, transcendentals=0
        ),
        name="two_steps",
    )(core, *ins)


def tie(value, *others):
    return lax.optimization_barrier((value,) + others)[0]


def local(field, atom_vel, cell_ids, fluid):
    ny = field.shape[2]
    count = lax.axis_size("gx") * lax.axis_size("gz")
    core = (lax.axis_index("gz") % 2).reshape(1)
    chip_pairs, far_pairs = [], []
    for i in range(0, count, 2):
        chip_pairs += [(i, i + 1), (i + 1, i)]
        far_pairs += [(i + 1, (i + 2) % count), ((i + 2) % count, i + 1)]

    def over_chip(block):
        return lax.ppermute(block, ROW_AXES, chip_pairs)

    def over_links(block):
        return lax.ppermute(block, ROW_AXES, far_pairs)

    def exchange(block):
        return lax.all_to_all(block, "gz", split_axis=0, concat_axis=0, tiled=True)

    first = over_links(field[:, :, LOW:FIRST])
    chip = over_chip(field)
    means, outgoing, *blocks = cell_means(
        atom_vel, cell_ids, fluid, field, (FIRST, SECOND, ny)
    )
    slab = exchange(outgoing)
    base = seed(slab, field)
    base_chip, base_far = over_chip(base), over_links(base)
    second = over_links(tie(blocks[0], base_chip, base_far, first, chip))
    low, returned = two_steps(
        core,
        [(base, 0), (field, 0, LOW)],
        [(base_chip, 0), (chip, 0, LOW)],
        [(base_far, 0), (first, LOW)],
        0,
        TILE,
        ny,
        whole=False,
    )
    back = exchange(returned)
    own, beside = [(field, 0)], [(chip, 0)]
    far = [(base_far, 0), (first, LOW), (second, FIRST)]
    third = over_links(tie(blocks[1], second, back))
    far.append((third, SECOND))
    new_atoms = constrain(atom_vel, cell_ids, fluid, back, means)
    start, reach = TILE, SECOND - TILE
    (part,) = two_steps(core, own, beside, far[:3], start, reach, ny, (40, 72, 104, 136))
    (new_field,) = two_steps(
        core, own, beside, far[2:], reach, ny, ny, (208, 232), into=part, low=low
    )
    return new_field, new_atoms


def solution(mesh):
    placed = (
        P(None, ("gx", "gz"), None, None),
        P(None, None, "gx", "gz"),
        P(None, "gx", "gz"),
        P(None, "gx", "gz"),
    )
    return jax.shard_map(
        local,
        mesh=mesh,
        in_specs=placed,
        out_specs=(P(None, ("gx", "gz"), None, None), P(None, None, "gx", "gz")),
        check_vma=False,
    )
```
